256 devices in a mesh: pair: 2 (over y_lo), lat: 128 (over z, x, y_hi, core).
Axes of the slice: x: 4, y: 4 (y_hi: 2, y_lo: 2; y = y_hi * 2 + y_lo), z: 8, core: 2. Of those that a mesh axis runs over, the one named last changes fastest.
Arguments:
- activations: bfloat16 [2, 256, 8192], P('pair', 'lat'), may hold values from -6 to 6
- enc_weight: bfloat16 [2, 16384, 8192], P('pair', 'lat'), may hold values from -0.046875 to 0.046875
- enc_bias: float32 [16384], P('lat'), may hold values from -3 to 3
- dec_weight: bfloat16 [2, 16384, 8192], P('pair', 'lat'), may hold values from -0.046875 to 0.046875
- dec_bias: float32 [2, 8192], P('pair'), may hold values from -6 to 6
- block_list: int32 [256], P('lat'), may hold values from 0 to 1, as said below
- block_count: int32 [128], P('lat'), may hold values from 1 to 2, as said below
Outputs:
- d_enc_weight: bfloat16 [2, 16384, 8192], P('pair', 'lat')
- d_dec_weight: bfloat16 [2, 16384, 8192], P('pair', 'lat')
- d_enc_bias: float32 [16384], P('lat')
- d_dec_bias: float32 [2, 8192], P('pair')
The draws below stay inside these ranges and needn't reach their ends.
Inputs may be any that keep to these rules, and one draw needn't show every extreme that they name: `block_list`: for each latent block, the first block_count entries of its list are distinct token blocks; the later entries are token blocks too and are not live. `block_count`: some latent block lists all 2 token blocks and some lists one.
All inputs are finite; a program needn't handle non-finite values.
Results may differ from the reference program's by a relative error of at most 0.0075.
Values may be sent and summed in bfloat16 or wider, within the bound.
No kernel may reach another device: no remote copies, remote signals or barrier semaphores. Data moves between devices by JAX's collectives and lax.ppermute only.
A program may use at most 128 MiB of HBM per device.

```python
import jax
import jax.numpy as jnp
from jax import lax

D = 8192
BLK = 128
LAT_DEV = 128
TOK_BLOCKS = 2
TOKENS = 256
LATENTS = 16384
N_LAT = 128


def draw_block_list(key, part):
    key = jax.random.fold_in(key, 11)
    scores = jax.random.randint(key, (N_LAT, TOK_BLOCKS), 0, 1 << 20)
    scores = scores * TOK_BLOCKS + jnp.arange(TOK_BLOCKS, dtype=jnp.int32)[None, :]
    return jnp.argsort(scores, axis=1, stable=True).astype(jnp.int32).reshape(-1)


def draw_block_count(key, part):
    key = jax.random.fold_in(key, 23)
    counts = jax.random.randint(key, (N_LAT,), 1, TOK_BLOCKS + 1)
    counts = counts.at[N_LAT - 1].set(1)
    counts = counts.at[0].set(TOK_BLOCKS)
    return counts.astype(jnp.int32)


def block_levels(stream_key, extent, split, low, largest):
    def one(dim, blocks):
        heights = jax.random.uniform(jax.random.fold_in(jax.random.fold_in(stream_key, 6), dim), (blocks,), jnp.float32, low / len(split), largest / len(split))
        return jnp.repeat(jnp.exp(heights), extent[dim] // blocks).reshape((-1,) + (1,) * (len(extent) - dim - 1))

    loudness = one(*split[0])
    for cut in split[1:]:
        loudness = loudness * one(*cut)
    return loudness


def noise(own_key, dims, spread, bound, shards=(), kind=jnp.bfloat16):
    entries = jax.random.normal(own_key, dims, jnp.float32) * spread
    if len(shards) > 0:
        entries = block_levels(own_key, dims, shards, -0.22, 0.18) * entries
    return jnp.clip(entries, min=-bound, max=bound).astype(kind)


def setup_inputs(seed: int = 0) -> dict:
    key_list = jax.random.split(jax.random.key(seed), 8)
    activations = noise(key_list[0], (2, TOKENS, D), 1.0, 6.0, ((0, 2), (1, 128)))
    enc_weight = noise(key_list[1], (2, LATENTS, D), (2 * D) ** -0.5, 0.046875, ((0, 2), (1, 128)))
    enc_bias = noise(key_list[2], (LATENTS,), 0.5, 3.0, ((0, 128),), jnp.float32)
    dec_weight = noise(key_list[3], (2, LATENTS, D), LATENTS ** -0.5, 0.046875, ((0, 2), (1, 128)))
    dec_bias = noise(key_list[4], (2, D), 1.0, 6.0, ((0, 2),), jnp.float32)
    block_list = draw_block_list(jax.random.fold_in(key_list[7], 71), 0)
    block_count = draw_block_count(jax.random.fold_in(key_list[7], 71), 0)
    return dict(activations=activations, enc_weight=enc_weight, enc_bias=enc_bias, dec_weight=dec_weight, dec_bias=dec_bias, block_list=block_list, block_count=block_count)


epsilon = 1e-06
sparsity = 0.25
loss_scale = 0.0625

def reference(activations, enc_weight, enc_bias, dec_weight, dec_bias, block_list, block_count):
    slot_table = block_list.reshape(N_LAT, TOK_BLOCKS)
    live_slot = jnp.arange(TOK_BLOCKS, dtype=jnp.int32)[None, :] < block_count[:, None]
    block_hits = (slot_table[:, :, None] == jnp.arange(TOK_BLOCKS, dtype=jnp.int32)[None, None, :]) & live_slot[:, :, None]
    block_mask = jnp.any(block_hits, axis=1).astype(jnp.float32)
    live_mask = jnp.repeat(jnp.repeat(block_mask.T, BLK, axis=0), LAT_DEV, axis=1)
    pre_act = jnp.dot(activations[0], enc_weight[0].T, preferred_element_type=jnp.float32)
    pre_act = pre_act + jnp.dot(activations[1], enc_weight[1].T, preferred_element_type=jnp.float32)
    pre_act = pre_act + enc_bias[None, :]
    latent_act = jax.nn.softplus(pre_act) * live_mask
    latent_low = latent_act.astype(jnp.bfloat16)
    row_norms = jnp.sqrt(lax.optimization_barrier(jnp.sum(jnp.square(dec_weight.astype(jnp.float32)), axis=2)) + epsilon)
    errors = []
    for which_model in range(2):
        rebuilt = jnp.dot(latent_low, dec_weight[which_model], preferred_element_type=jnp.float32) + dec_bias[which_model][None, :]
        errors.append((loss_scale * (rebuilt - activations[which_model].astype(jnp.float32))).astype(jnp.bfloat16))
    grad_latent = jnp.dot(errors[0], dec_weight[0].T, preferred_element_type=jnp.float32)
    grad_latent = grad_latent + jnp.dot(errors[1], dec_weight[1].T, preferred_element_type=jnp.float32)
    grad_latent = (grad_latent + loss_scale * sparsity * (row_norms[0] + row_norms[1])[None, :]) * live_mask
    pre_grad = grad_latent * jax.nn.sigmoid(pre_act)
    pre_low = pre_grad.astype(jnp.bfloat16)
    act_total = lax.optimization_barrier(jnp.sum(latent_act, axis=0))
    d_enc = jnp.stack([jnp.dot(pre_low.T, activations[which_model], preferred_element_type=jnp.float32) for which_model in range(2)]).astype(jnp.bfloat16)
    d_dec = jnp.stack([jnp.dot(latent_low.T, errors[which_model], preferred_element_type=jnp.float32) + loss_scale * sparsity * act_total[:, None] * dec_weight[which_model].astype(jnp.float32) / row_norms[which_model][:, None] for which_model in range(2)]).astype(jnp.bfloat16)
    d_enc_bias = lax.optimization_barrier(jnp.sum(pre_grad, axis=0))
    d_dec_bias = jnp.stack([lax.optimization_barrier(jnp.sum(errors[which_model].astype(jnp.float32), axis=0)) for which_model in range(2)])
    return (d_enc, d_dec, d_enc_bias, d_dec_bias)
```

```python
import jax
import jax.numpy as jnp
from jax import lax
from jax.sharding import PartitionSpec as P

BLK = 128
NZ, NX, NY, NC = 8, 4, 2, 2

epsilon = 1e-06
sparsity = 0.25
loss_scale = 0.0625


def place(z, x, y, c):
    return (((z % NZ) * NX + x % NX) * NY + y % NY) * NC + c % NC


def fetch(value, z=0, x=0, y=0, c=0):
    pairs = [
        (place(iz + z, ix + x, iy + y, ic + c), place(iz, ix, iy, ic))
        for iz in range(NZ)
        for ix in range(NX)
        for iy in range(NY)
        for ic in range(NC)
    ]
    return lax.ppermute(value, "lat", pairs)


def gather_rows(own):
    half = own.shape[1] // 2
    other = fetch(own, y=1)
    a2 = jnp.concatenate([own[0:1], other[0:1]], axis=0)
    b2 = jnp.concatenate([own[1:2], other[1:2]], axis=0)
    a8 = jnp.concatenate([a2] + [fetch(a2, x=k) for k in range(1, NX)], axis=0)
    b16 = jnp.concatenate([b2] + [fetch(b2, z=k) for k in range(1, NZ)], axis=0)
    up, down = a8, a8
    ups, downs = [], []
    for _ in range(3):
        up, down = fetch(up, z=1), fetch(down, z=-1)
        ups.append(up)
        downs.append(down)
    far = jnp.concatenate([fetch(up[:, :half], z=1), fetch(down[:, half:], z=-1)], axis=1)
    near, back = fetch(b16, x=1), fetch(b16, x=-1)
    opposite = jnp.concatenate([fetch(near[:, :half], x=1), fetch(back[:, half:], x=-1)], axis=1)
    mine = jnp.concatenate([a8] + ups + [far] + downs[::-1] + [b16, near, opposite, back], axis=0)
    return jnp.concatenate([mine, fetch(mine, c=1)], axis=0)


def low(value):
    return value.astype(jnp.bfloat16)


def add(value, arrived):
    return value + arrived.astype(jnp.float32)


def scatter_rows(part):
    rows, width = part.shape
    half = width // 2
    mine = add(part[: rows // 2], fetch(low(part[rows // 2 :]), c=1))
    a = [mine[8 * k : 8 * k + 8] for k in range(8)]
    b = [mine[64 + 16 * k : 80 + 16 * k] for k in range(4)]
    left, right = fetch(low(a[4][:, :half]), z=-1), fetch(low(a[4][:, half:]), z=1)
    up = jnp.concatenate([add(a[3][:, :half], left), a[3][:, half:]], axis=1)
    down = jnp.concatenate([a[5][:, :half], add(a[5][:, half:], right)], axis=1)
    for k in (2, 1):
        up, down = add(a[k], fetch(low(up), z=-1)), add(a[8 - k], fetch(low(down), z=1))
    a8 = add(add(a[0], fetch(low(up), z=-1)), fetch(low(down), z=1))
    left, right = fetch(low(b[2][:, :half]), x=-1), fetch(low(b[2][:, half:]), x=1)
    up = jnp.concatenate([add(b[1][:, :half], left), b[1][:, half:]], axis=1)
    down = jnp.concatenate([b[3][:, :half], add(b[3][:, half:], right)], axis=1)
    b16 = add(add(b[0], fetch(low(up), x=-1)), fetch(low(down), x=1))
    a2 = a8[0:2]
    for k in range(1, NX):
        a2 = add(a2, fetch(low(a8[2 * k : 2 * k + 2]), x=-k))
    b2 = b16[0:2]
    for k in range(1, NZ):
        b2 = add(b2, fetch(low(b16[2 * k : 2 * k + 2]), z=-k))
    own = jnp.concatenate([a2[0:1], b2[0:1]], axis=0)
    return own + fetch(jnp.concatenate([a2[1:2], b2[1:2]], axis=0), y=1)


def swap_pair(value):
    return lax.ppermute(value, "pair", [(0, 1), (1, 0)])


def dot(left, right, over):
    return lax.dot_general(left, right, ((over[:1], over[1:]), ((), ())), preferred_element_type=jnp.float32)


def on_device(activations, enc_weight, enc_bias, dec_weight, dec_bias, block_list, block_count):
    enc, dec = enc_weight[0], dec_weight[0]
    own = activations[0]
    act = gather_rows(own)
    tokens = act.shape[0]

    row = jnp.arange(tokens, dtype=jnp.int32) % 128
    z_off = jnp.where(row < 64, row // 8, (row % 16) // 2)
    z_row = (lax.axis_index("lat") // (NX * NY * NC) + z_off) % NZ
    block = z_row * (2 * NX * NY * NC) // BLK
    slots = jnp.arange(block_list.shape[0], dtype=jnp.int32) < block_count[0]
    live = jnp.any((block[:, None] == block_list[None, :]) & slots[None, :], axis=1)
    live = live.astype(jnp.float32)[:, None]

    norm_own = jnp.sqrt(jnp.sum(jnp.square(dec.astype(jnp.float32)), axis=1) + epsilon)
    pre_part = dot(act, enc, (1, 1))
    packed = jnp.concatenate([pre_part, jnp.broadcast_to(norm_own[None, :], (8, norm_own.shape[0]))], axis=0)
    packed = packed + swap_pair(packed)
    norm_sum = packed[tokens : tokens + 1]
    pre_act = packed[:tokens] + enc_bias[None, :]
    latent_act = jax.nn.softplus(pre_act) * live
    latent_low = low(latent_act)

    rebuilt = scatter_rows(dot(latent_low, dec, (1, 0))) + dec_bias
    err = gather_rows(low(loss_scale * (rebuilt - own.astype(jnp.float32))))

    grad_part = dot(err, dec, (1, 1))
    grad_sum = grad_part + swap_pair(grad_part)
    grad_latent = (grad_sum + loss_scale * sparsity * norm_sum) * live
    pre_grad = grad_latent * jax.nn.sigmoid(pre_act)
    pre_low = low(pre_grad)

    act_total = jnp.sum(latent_act, axis=0)
    d_dec = dot(latent_low, err, (0, 0))
    d_dec = d_dec + (loss_scale * sparsity * act_total / norm_own)[:, None] * dec.astype(jnp.float32)
    d_dec_bias = dot(jnp.ones((8, tokens), jnp.bfloat16), err, (1, 0))[0:1]
    d_enc = dot(pre_low, act, (0, 0))
    d_enc_bias = jnp.sum(pre_grad, axis=0)
    return low(d_enc)[None], low(d_dec)[None], d_enc_bias, d_dec_bias


def solution(mesh):
    placed = (
        P("pair", "lat", None),
        P("pair", "lat", None),
        P("lat"),
        P("pair", "lat", None),
        P("pair", None),
        P("lat"),
        P("lat"),
    )
    return jax.shard_map(
        on_device,
        mesh=mesh,
        in_specs=placed,
        out_specs=(P("pair", "lat", None), P("pair", "lat", None), P("lat"), P("pair", None)),
        check_vma=False,
    )
```

```python
import jax
import jax.numpy as jnp
import numpy as np
from jax import lax
from jax.experimental import pallas as pl
from jax.experimental.pallas import tpu as pltpu
from jax.sharding import PartitionSpec as P

BLK = 128
NZ, NX, NY, NC = 8, 4, 2, 2

epsilon = 1e-06
sparsity = 0.25
loss_scale = 0.0625

COLUMNS = ((0, 0), (0, 2), (0, 1), (0, -1), (-1, -1), (1, 1), (-1, 0), (1, 2))
ROW_Z = np.array([dz + 2 * k for _ in range(NC) for dz, _ in COLUMNS for k in range(4) for _ in range(4)], np.int32)


def place(z, x, y, c):
    return (((z % NZ) * NX + x % NX) * NY + y % NY) * NC + c % NC


def fetch(value, z=0, x=0, y=0, c=0):
    pairs = [
        (place(iz + z, ix + x, iy + y, ic + c), place(iz, ix, iy, ic))
        for iz in range(NZ)
        for ix in range(NX)
        for iy in range(NY)
        for ic in range(NC)
    ]
    return lax.ppermute(value, "lat", pairs)


def pack(pieces):
    rows = [piece.shape[0] for piece in pieces]

    def kernel(*refs):
        at = 0
        for ref, count in zip(refs[:-1], rows):
            refs[-1][at : at + count, :] = ref[...]
            at += count

    return pl.pallas_call(
        kernel,
        out_shape=jax.ShapeDtypeStruct((sum(rows), pieces[0].shape[1]), pieces[0].dtype),
        in_specs=[pl.BlockSpec(memory_space=pltpu.VMEM)] * len(pieces),
        out_specs=pl.BlockSpec(memory_space=pltpu.VMEM),
        compiler_params=pltpu.CompilerParams(vmem_limit_bytes=32 * 1024 * 1024),
    )(*pieces)


def gather_rows(own):
    four = jnp.concatenate([own, fetch(own, y=1)], axis=0)
    column = jnp.concatenate([four] + [fetch(four, z=k) for k in (2, 4, 6)], axis=0)
    two = fetch(column, x=2)
    first = pack([column, two, fetch(column, x=1), fetch(column, x=-1)])
    second = pack(
        [fetch(column, z=-1, x=-1), fetch(column, z=1, x=1), fetch(column, z=-1), fetch(two, z=1)]
    )
    return pack([first, second, fetch(first, c=1), fetch(second, c=1)])


def low(value):
    return value.astype(jnp.bfloat16)


def add(value, arrived):
    return value + arrived.astype(jnp.float32)


def scatter_rows(latent, dec):
    rows = latent.shape[0] // 2
    theirs = low(dot(latent[rows:], dec, (1, 0)))
    mine = add(dot(latent[:rows], dec, (1, 0)), fetch(theirs, c=1))
    c, two, up, down, diag, other, back, far = [mine[16 * k : 16 * k + 16] for k in range(8)]
    two = add(two, fetch(low(far), z=-1))
    c = add(c, fetch(low(up), x=-1))
    c = add(c, fetch(low(down), x=1))
    c = add(c, fetch(low(diag), z=1, x=1))
    c = add(c, fetch(low(other), z=-1, x=-1))
    c = add(c, fetch(low(back), z=1))
    c = add(c, fetch(low(two), x=2))
    four = c[0:4]
    for k in (1, 2, 3):
        four = add(four, fetch(low(c[4 * k : 4 * k + 4]), z=-2 * k))
    return four[0:2] + fetch(four[2:4], y=1)


def swap_pair(value):
    return lax.ppermute(value, "pair", [(0, 1), (1, 0)])


def dot(left, right, over):
    return lax.dot_general(left, right, ((over[:1], over[1:]), ((), ())), preferred_element_type=jnp.float32)


def on_device(activations, enc_weight, enc_bias, dec_weight, dec_bias, block_list, block_count):
    enc, dec = enc_weight[0], dec_weight[0]
    own = activations[0]
    act = gather_rows(own)
    tokens = act.shape[0]

    z_row = (lax.axis_index("lat") // (NX * NY * NC) + ROW_Z) % NZ
    block = z_row * (2 * NX * NY * NC) // BLK
    slots = jnp.arange(block_list.shape[0], dtype=jnp.int32) < block_count[0]
    live = jnp.any((block[:, None] == block_list[None, :]) & slots[None, :], axis=1)
    live = live.astype(jnp.float32)[:, None]

    norm_own = jnp.sqrt(jnp.sum(jnp.square(dec.astype(jnp.float32)), axis=1) + epsilon)
    pre_part = dot(act, enc, (1, 1))
    packed = jnp.concatenate([pre_part, jnp.broadcast_to(norm_own[None, :], (8, norm_own.shape[0]))], axis=0)
    packed = packed + swap_pair(packed)
    norm_sum = packed[tokens : tokens + 1]
    pre_act = packed[:tokens] + enc_bias[None, :]
    latent_act = jax.nn.softplus(pre_act) * live
    latent_low = low(latent_act)

    rebuilt = scatter_rows(latent_low, dec) + dec_bias
    err = gather_rows(low(loss_scale * (rebuilt - own.astype(jnp.float32))))

    grad_part = dot(err, dec, (1, 1))
    grad_sum = grad_part + swap_pair(grad_part)
    grad_latent = (grad_sum + loss_scale * sparsity * norm_sum) * live
    pre_grad = grad_latent * jax.nn.sigmoid(pre_act)
    pre_low = low(pre_grad)

    act_total = jnp.sum(latent_act, axis=0)
    d_dec = dot(latent_low, err, (0, 0))
    d_dec = d_dec + (loss_scale * sparsity * act_total / norm_own)[:, None] * dec.astype(jnp.float32)
    d_dec_bias = dot(jnp.ones((8, tokens), jnp.bfloat16), err, (1, 0))[0:1]
    d_enc = dot(pre_low, act, (0, 0))
    d_enc_bias = jnp.sum(pre_grad, axis=0)
    return low(d_enc)[None], low(d_dec)[None], d_enc_bias, d_dec_bias


def solution(mesh):
    placed = (
        P("pair", "lat", None),
        P("pair", "lat", None),
        P("lat"),
        P("pair", "lat", None),
        P("pair", None),
        P("lat"),
        P("lat"),
    )
    return jax.shard_map(
        on_device,
        mesh=mesh,
        in_specs=placed,
        out_specs=(P("pair", "lat", None), P("pair", "lat", None), P("lat"), P("pair", None)),
        check_vma=False,
    )
```

```python
import jax
import jax.numpy as jnp
import numpy as np
from jax import lax
from jax.experimental import pallas as pl
from jax.experimental.pallas import tpu as pltpu
from jax.sharding import PartitionSpec as P

BLK = 128
NZ, NX, NY, NC = 8, 4, 2, 2

epsilon = 1e-06
sparsity = 0.25
loss_scale = 0.0625

ROW_BLOCK = np.arange(2 * BLK) % 8 // 4


def place(z, x, y, c):
    return (((z % NZ) * NX + x % NX) * NY + y % NY) * NC + c % NC


def fetch(value, z=0, x=0, y=0, c=0, mirror=False):
    pairs = []
    for iz in range(NZ):
        for ix in range(NX):
            for iy in range(NY):
                for ic in range(NC):
                    sign = -1 if mirror and ic == 1 else 1
                    pairs.append((place(iz + sign * z, ix + sign * x, iy + y, ic + c), place(iz, ix, iy, ic)))
    return lax.ppermute(value, "lat", pairs)


def pack(pieces):
    rows = [piece.shape[0] for piece in pieces]

    def kernel(*refs):
        at = 0
        for ref, count in zip(refs[:-1], rows):
            refs[-1][at : at + count, :] = ref[...]
            at += count

    return pl.pallas_call(
        kernel,
        out_shape=jax.ShapeDtypeStruct((sum(rows), pieces[0].shape[1]), pieces[0].dtype),
        in_specs=[pl.BlockSpec(memory_space=pltpu.VMEM)] * len(pieces),
        out_specs=pl.BlockSpec(memory_space=pltpu.VMEM),
        compiler_params=pltpu.CompilerParams(vmem_limit_bytes=32 * 1024 * 1024),
    )(*pieces)


def by_z(value):
    near = [value] + [fetch(value, z=k) for k in (2, 4, 6)]
    turn = lax.axis_index("lat") // (2 * NX * NY * NC)
    return [lax.select_n(turn, *[near[(k - first) % 4] for first in range(4)]) for k in range(4)]


AROUND = (dict(x=1), dict(z=1), dict(x=1, z=1))
BACK = (dict(x=-1), dict(z=-1), dict(x=-1, z=-1))


def gather_rows(octet):
    group = pack([octet, fetch(octet, y=1), fetch(octet, x=2), fetch(octet, x=2, y=1)])
    groups = [group] + [fetch(group, mirror=True, **to) for to in AROUND]
    return groups + [fetch(each, c=1) for each in groups]


def low(value):
    return value.astype(jnp.bfloat16)


def add(value, arrived):
    return value + arrived.astype(jnp.float32)


def scatter_rows(latent, dec):
    rows = latent.shape[0] // 2
    theirs = low(dot(latent[rows:], dec, (1, 0)))
    mine = dot(latent[:rows], dec, (1, 0))
    groups = [add(mine[at : at + 32], fetch(theirs[at : at + 32], c=1)) for at in (96, 64, 32, 0)][::-1]
    group = groups[0]
    for each, to in zip(groups[:0:-1], BACK[::-1]):
        group = add(group, fetch(low(each), mirror=True, **to))
    octet = add(group[0:8], fetch(low(group[8:16]), y=1))
    octet = add(octet, fetch(low(group[16:24]), x=2))
    octet = add(octet, fetch(low(group[24:32]), x=2, y=1))
    parts = [part.astype(jnp.float32) for part in by_z(low(octet))]
    return parts[0] + parts[1] + parts[2] + parts[3]


def swap_pair(value):
    return lax.ppermute(value, "pair", [(0, 1), (1, 0)])


def dot(left, right, over):
    return lax.dot_general(left, right, ((over[:1], over[1:]), ((), ())), preferred_element_type=jnp.float32)


def on_device(activations, enc_weight, enc_bias, dec_weight, dec_bias, block_list, block_count):
    enc, dec = enc_weight[0], dec_weight[0]
    own = activations[0]
    tokens = 2 * BLK
    norm_own = jnp.sqrt(jnp.sum(jnp.square(dec.astype(jnp.float32)), axis=1) + epsilon)
    own_octet = jnp.concatenate(by_z(own), axis=0)
    act_groups = gather_rows(own_octet)

    slots = jnp.arange(block_list.shape[0], dtype=jnp.int32) < block_count[0]
    live = jnp.any((ROW_BLOCK[:, None] == block_list[None, :]) & slots[None, :], axis=1)
    live = live.astype(jnp.float32)[:, None]

    act_halves = [pack(act_groups[:4]), pack(act_groups[4:])]
    pre_part = [dot(half, enc, (1, 1)) for half in act_halves]
    packed = jnp.concatenate(pre_part + [jnp.broadcast_to(norm_own[None, :], (8, norm_own.shape[0]))], axis=0)
    arrived, act = lax.optimization_barrier((swap_pair(packed), pack(act_halves)))
    packed = packed + arrived
    norm_sum = packed[tokens : tokens + 1]
    pre_act = packed[:tokens] + enc_bias[None, :]
    latent_act = jax.nn.softplus(pre_act) * live
    latent_low = low(latent_act)

    rebuilt = scatter_rows(latent_low, dec) + dec_bias
    err_groups = gather_rows(low(loss_scale * (rebuilt - own_octet.astype(jnp.float32))))

    err_halves = [pack(err_groups[:4]), pack(err_groups[4:])]
    grad_part = jnp.concatenate([dot(half, dec, (1, 1)) for half in err_halves], axis=0)
    err = pack(err_halves)
    act_total = jnp.sum(latent_act, axis=0)
    d_dec = dot(latent_low, err, (0, 0))
    d_dec = d_dec + (loss_scale * sparsity * act_total / norm_own)[:, None] * dec.astype(jnp.float32)
    d_dec_bias = dot(jnp.ones((8, tokens), jnp.bfloat16), err, (1, 0))[0:1]
    arrived, d_dec, d_dec_bias = lax.optimization_barrier((swap_pair(grad_part), low(d_dec), d_dec_bias))
    grad_sum = grad_part + arrived
    grad_latent = (grad_sum + loss_scale * sparsity * norm_sum) * live
    pre_grad = grad_latent * jax.nn.sigmoid(pre_act)
    pre_low = low(pre_grad)

    d_enc = dot(pre_low, act, (0, 0))
    d_enc_bias = jnp.sum(pre_grad, axis=0)
    return low(d_enc)[None], d_dec[None], d_enc_bias, d_dec_bias


def solution(mesh):
    placed = (
        P("pair", "lat", None),
        P("pair", "lat", None),
        P("lat"),
        P("pair", "lat", None),
        P("pair", None),
        P("lat"),
        P("lat"),
    )
    return jax.shard_map(
        on_device,
        mesh=mesh,
        in_specs=placed,
        out_specs=(P("pair", "lat", None), P("pair", "lat", None), P("lat"), P("pair", None)),
        check_vma=False,
    )
```

```python
import jax
import jax.numpy as jnp
import numpy as np
from jax import lax
from jax.experimental import pallas as pl
from jax.experimental.pallas import tpu as pltpu
from jax.sharding import PartitionSpec as P

BLK = 128
NZ, NX, NY, NC = 8, 4, 2, 2

epsilon = 1e-06
sparsity = 0.25
loss_scale = 0.0625

EVEN_Z = ((0, 0, 0), (2, 0, 0), (6, 0, 0), (4, 0, 0))
EVEN_XY = ((0, 0, 0), (0, 0, 1), (0, 2, 0), (0, 2, 1))
TURNS = [[(0, 1, 3, 2)[(i - own) % 4] for i in range(4)] for own in range(4)]
TURNS += [[i ^ own for i in range(4)] for own in range(4)]
OCTET_Z = np.array([dz + 2 * k for dz in (0, 0, -1, -1) for k in (0, 1, 3, 2)], np.int32)


def place(z, x, y, c):
    return (((z % NZ) * NX + x % NX) * NY + y % NY) * NC + c % NC


def fetch(value, *offsets, c=0):
    pairs = []
    for iz in range(NZ):
        for ix in range(NX):
            for iy in range(NY):
                for ic in range(NC):
                    z, x, y = offsets[ic % len(offsets)]
                    pairs.append((place(iz + z, ix + x, iy + y, ic + c), place(iz, ix, iy, ic)))
    return lax.ppermute(value, "lat", pairs)


def swap_core(value):
    return fetch(value, (0, 0, 0), c=1)


def pack(pieces):
    rows = [piece.shape[0] for piece in pieces]

    def kernel(*refs):
        at = 0
        for ref, count in zip(refs[:-1], rows):
            refs[-1][at : at + count, :] = ref[...]
            at += count

    return pl.pallas_call(
        kernel,
        out_shape=jax.ShapeDtypeStruct((sum(rows), pieces[0].shape[1]), pieces[0].dtype),
        in_specs=[pl.BlockSpec(memory_space=pltpu.VMEM)] * len(pieces),
        out_specs=pl.BlockSpec(memory_space=pltpu.VMEM),
        compiler_params=pltpu.CompilerParams(vmem_limit_bytes=32 * 1024 * 1024),
    )(*pieces)


def position():
    at = lax.axis_index("lat")
    return at // (NX * NY * NC), at // (NY * NC) % NX, at // NC % NY, at % NC


def by_partner(value):
    near = [value] + [fetch(value, EVEN_Z[k], EVEN_XY[k]) for k in (1, 2, 3)]
    z, x, y, core = position()
    own = jnp.where(core == 0, z // 2, 4 + x // 2 * 2 + y)
    return [lax.select_n(own, *[near[turn[i]] for turn in TURNS]) for i in range(4)]


AROUND = (((0, 1, 0), (0, -1, 0)), ((1, 0, 0), (-1, 0, 0)), ((1, 1, 0), (-1, -1, 0)))


def gather_rows(octet):
    group = pack([octet] + [fetch(octet, EVEN_XY[k], EVEN_Z[k]) for k in (1, 2, 3)])
    groups = [group] + [fetch(group, *to) for to in AROUND]
    return groups + [swap_core(each) for each in groups]


def low(value):
    return value.astype(jnp.bfloat16)


def add(value, arrived):
    return value + arrived.astype(jnp.float32)


def scatter_rows(latent, dec):
    rows = latent.shape[0] // 2
    theirs = low(dot(latent[rows:], dec, (1, 0)))
    mine = dot(latent[:rows], dec, (1, 0))
    sent = low(add(mine[96:], swap_core(theirs[96:])))
    theirs, sent = lax.optimization_barrier((theirs[:96], sent))
    rest = add(mine[:96], swap_core(theirs))
    group = add(rest[:32], fetch(sent, *AROUND[2][::-1]))
    group = add(group, fetch(low(rest[64:]), *AROUND[1][::-1]))
    group = add(group, fetch(low(rest[32:64]), *AROUND[0][::-1]))
    octet = group[0:8]
    for k, back in ((3, 3), (2, 1), (1, 2)):
        octet = add(octet, fetch(low(group[8 * k : 8 * k + 8]), EVEN_XY[k], EVEN_Z[back]))
    parts = [part.astype(jnp.float32) for part in by_partner(low(octet))]
    return parts[0] + parts[1] + parts[2] + parts[3]


def swap_pair(value):
    return lax.ppermute(value, "pair", [(0, 1), (1, 0)])


def dot(left, right, over):
    return lax.dot_general(left, right, ((over[:1], over[1:]), ((), ())), preferred_element_type=jnp.float32)


def on_device(activations, enc_weight, enc_bias, dec_weight, dec_bias, block_list, block_count):
    enc, dec = enc_weight[0], dec_weight[0]
    own = activations[0]
    tokens = 2 * BLK
    norm_own = jnp.sqrt(jnp.sum(jnp.square(dec.astype(jnp.float32)), axis=1) + epsilon)
    own_octet = jnp.concatenate(by_partner(own), axis=0)
    act_groups = gather_rows(own_octet)

    slots = jnp.arange(block_list.shape[0], dtype=jnp.int32) < block_count[0]
    z, _, _, core = position()
    by_octet = jnp.repeat((z + OCTET_Z) % NZ, 8)
    kinds = [jnp.tile(jnp.arange(NZ, dtype=jnp.int32), tokens // 2 // NZ), by_octet]
    z_row = jnp.concatenate([jnp.where(core == own, kinds[0], kinds[1]) for own in (0, 1)])
    block = z_row // (NZ // 2)
    live = jnp.any((block[:, None] == block_list[None, :]) & slots[None, :], axis=1)
    live = live.astype(jnp.float32)[:, None]

    act_halves = [pack(act_groups[:4]), pack(act_groups[4:])]
    pre_part = [dot(half, enc, (1, 1)) for half in act_halves]
    packed = jnp.concatenate(pre_part + [jnp.broadcast_to(norm_own[None, :], (8, norm_own.shape[0]))], axis=0)
    arrived, act = lax.optimization_barrier((swap_pair(low(packed)), pack(act_halves)))
    packed = add(packed, arrived)
    norm_sum = packed[tokens : tokens + 1]
    pre_act = packed[:tokens] + enc_bias[None, :]
    latent_act = jax.nn.softplus(pre_act) * live
    latent_low = low(latent_act)

    rebuilt = scatter_rows(latent_low, dec) + dec_bias
    err_groups = gather_rows(low(loss_scale * (rebuilt - own_octet.astype(jnp.float32))))

    err_halves = [pack(err_groups[:4]), pack(err_groups[4:])]
    grad_part = jnp.concatenate([dot(half, dec, (1, 1)) for half in err_halves], axis=0)
    err = pack(err_halves)
    act_total = jnp.sum(latent_act, axis=0)
    d_dec = dot(latent_low, err, (0, 0))
    d_dec = d_dec + (loss_scale * sparsity * act_total / norm_own)[:, None] * dec.astype(jnp.float32)
    d_dec_bias = dot(jnp.ones((8, tokens), jnp.bfloat16), err, (1, 0))[0:1]
    arrived, d_dec, d_dec_bias = lax.optimization_barrier((swap_pair(low(grad_part)), low(d_dec), d_dec_bias))
    grad_sum = add(grad_part, arrived)
    grad_latent = (grad_sum + loss_scale * sparsity * norm_sum) * live
    pre_grad = grad_latent * jax.nn.sigmoid(pre_act)
    pre_low = low(pre_grad)

    d_enc = dot(pre_low, act, (0, 0))
    d_enc_bias = jnp.sum(pre_grad, axis=0)
    return low(d_enc)[None], d_dec[None], d_enc_bias, d_dec_bias


def solution(mesh):
    placed = (
        P("pair", "lat", None),
        P("pair", "lat", None),
        P("lat"),
        P("pair", "lat", None),
        P("pair", None),
        P("lat"),
        P("lat"),
    )
    return jax.shard_map(
        on_device,
        mesh=mesh,
        in_specs=placed,
        out_specs=(P("pair", "lat", None), P("pair", "lat", None), P("lat"), P("pair", None)),
        check_vma=False,
    )
```

```python
import jax
import jax.numpy as jnp
import numpy as np
from jax import lax
from jax.experimental import pallas as pl
from jax.experimental.pallas import tpu as pltpu
from jax.sharding import PartitionSpec as P

BLK = 128
NZ, NX, NY, NC = 8, 4, 2, 2

epsilon = 1e-06
sparsity = 0.25
loss_scale = 0.0625

EVEN_Z = ((0, 0, 0), (2, 0, 0), (6, 0, 0), (4, 0, 0))
EVEN_XY = ((0, 0, 0), (0, 0, 1), (0, 2, 0), (0, 2, 1))
TURNS = [[(0, 1, 3, 2)[(i - own) % 4] for i in range(4)] for own in range(4)]
TURNS += [[i ^ own for i in range(4)] for own in range(4)]
OCTET_Z = np.array([dz + 2 * k for dz in (0, -1, -1, 0) for k in (0, 2, 3, 1)], np.int32)


def place(z, x, y, c):
    return (((z % NZ) * NX + x % NX) * NY + y % NY) * NC + c % NC


def fetch(value, *offsets, c=0):
    pairs = []
    for iz in range(NZ):
        for ix in range(NX):
            for iy in range(NY):
                for ic in range(NC):
                    z, x, y = offsets[ic % len(offsets)]
                    pairs.append((place(iz + z, ix + x, iy + y, ic + c), place(iz, ix, iy, ic)))
    return lax.ppermute(value, "lat", pairs)


def swap_core(value):
    return fetch(value, (0, 0, 0), c=1)


def pack(pieces):
    rows = [piece.shape[0] for piece in pieces]

    def kernel(*refs):
        at = 0
        for ref, count in zip(refs[:-1], rows):
            refs[-1][at : at + count, :] = ref[...]
            at += count

    return pl.pallas_call(
        kernel,
        out_shape=jax.ShapeDtypeStruct((sum(rows), pieces[0].shape[1]), pieces[0].dtype),
        in_specs=[pl.BlockSpec(memory_space=pltpu.VMEM)] * len(pieces),
        out_specs=pl.BlockSpec(memory_space=pltpu.VMEM),
        compiler_params=pltpu.CompilerParams(vmem_limit_bytes=32 * 1024 * 1024),
    )(*pieces)


def position():
    at = lax.axis_index("lat")
    return at // (NX * NY * NC), at // (NY * NC) % NX, at // NC % NY, at % NC


def by_partner(value):
    near = [value] + [fetch(value, EVEN_Z[k], EVEN_XY[k]) for k in (1, 2, 3)]
    z, x, y, core = position()
    own = jnp.where(core == 0, z // 2, 4 + x // 2 * 2 + y)
    return [lax.select_n(own, *[near[turn[i]] for turn in TURNS]) for i in range(4)]


AROUND = (((1, 1, 0), (-1, -1, 0)), ((1, 0, 0), (-1, 0, 0)), ((0, 1, 0), (0, -1, 0)))


def after(value, *earlier):
    return lax.optimization_barrier((value,) + earlier)


def gather_rows(octet, *beside):
    group = pack([octet] + [fetch(octet, EVEN_XY[k], EVEN_Z[k]) for k in (3, 2, 1)])
    group, *beside = after(group, *beside)
    return [group] + [fetch(group, *to) for to in AROUND], beside


def low(value):
    return value.astype(jnp.bfloat16)


def add(value, arrived):
    return value + arrived.astype(jnp.float32)


def scatter_rows(terms):
    group = terms[:32]
    for k in (3, 2, 1):
        group = add(group, fetch(low(terms[32 * k : 32 * k + 32]), *AROUND[k - 1][::-1]))
    octet = group[0:8]
    for at, k, back in ((3, 1, 2), (2, 2, 1), (1, 3, 3)):
        octet = add(octet, fetch(low(group[8 * at : 8 * at + 8]), EVEN_XY[k], EVEN_Z[back]))
    parts = [part.astype(jnp.float32) for part in by_partner(low(octet))]
    return parts[0] + parts[1] + parts[2] + parts[3]


def swap_pair(value):
    return lax.ppermute(value, "pair", [(0, 1), (1, 0)])


def dot(left, right, over):
    return lax.dot_general(left, right, ((over[:1], over[1:]), ((), ())), preferred_element_type=jnp.float32)


def total_rows(groups):
    rows = pack(groups) if len(groups) > 1 else groups[0]
    return dot(jnp.ones((8, rows.shape[0]), rows.dtype), rows, (1, 0))[0:1]


def on_device(activations, enc_weight, enc_bias, dec_weight, dec_bias, block_list, block_count):
    enc, dec = enc_weight[0], dec_weight[0]
    own = activations[0]
    own_octet, enc_other = after(jnp.concatenate(by_partner(own), axis=0), swap_core(enc))
    act_groups, (dec_other,) = gather_rows(own_octet, swap_core(dec))
    norm_own = jnp.sqrt(jnp.sum(jnp.square(dec.astype(jnp.float32)), axis=1) + epsilon)

    lats = enc.shape[0]
    slots = jnp.arange(block_list.shape[0], dtype=jnp.int32) < block_count[0]
    hits = jnp.arange(2, dtype=jnp.int32)[:, None] == block_list[None, :]
    hits = jnp.any(hits & slots[None, :], axis=1).astype(jnp.float32)[:, None]
    facts = [enc_bias[None, :], jnp.broadcast_to(hits, (2, lats)), norm_own[None, :], jnp.zeros((4, lats), jnp.float32)]
    facts = jnp.concatenate(facts, axis=0)
    facts = jnp.concatenate([facts, swap_core(facts)], axis=1)
    both_enc, both_dec = pack([enc, enc_other]), pack([dec, dec_other])
    z, _, _, core = position()
    kinds = [jnp.tile(jnp.arange(NZ, dtype=jnp.int32), BLK // NZ), jnp.repeat((z + OCTET_Z) % NZ, 8)]
    block = jnp.where(core == 0, kinds[0], kinds[1]) // (NZ // 2)
    live = jnp.where(block[:, None] == 0, facts[1:2], facts[2:3])

    act = pack(act_groups)
    pre_part = dot(act, both_enc, (1, 1))
    act, pre_part = after(act, pre_part)
    act_other = swap_core(act)
    packed = jnp.concatenate([pre_part, jnp.broadcast_to(facts[3:4], (16, 2 * lats))], axis=0)
    packed = add(packed, swap_pair(low(packed)))
    norm_sum = packed[BLK : BLK + 1]
    pre_act = packed[:BLK] + facts[0:1]
    latent_act = jax.nn.softplus(pre_act) * live
    rebuilt = scatter_rows(dot(low(latent_act), both_dec, (1, 0)))

    other_block = jnp.where(core == 0, kinds[1], kinds[0]) // (NZ // 2)
    other_live = jnp.where(other_block[:, None] == 0, facts[1:2, :lats], facts[2:3, :lats])
    live = jnp.concatenate([live[:, :lats], other_live], axis=0)
    pre_act = jnp.concatenate([pre_act[:, :lats], swap_core(pre_act[:, lats:])], axis=0)
    latents = jax.nn.softplus(pre_act) * live
    slope = loss_scale * sparsity * jnp.sum(latents, axis=0) / norm_own
    factor = jax.nn.sigmoid(pre_act) * live
    rebuilt, act, latents, slope, factor = lax.optimization_barrier(
        (rebuilt + dec_bias, pack([act, act_other]), low(latents), slope, factor)
    )
    err_groups, _ = gather_rows(low(loss_scale * (rebuilt - own_octet.astype(jnp.float32))))
    halves = [pack(err_groups), pack([swap_core(group) for group in err_groups])]
    grad_part = jnp.concatenate([dot(half, dec, (1, 1)) for half in halves], axis=0)
    err = pack(halves)
    d_dec = dot(latents, err, (0, 0)) + slope[:, None] * dec.astype(jnp.float32)
    d_dec_bias = total_rows([err])
    arrived, d_dec, d_dec_bias = lax.optimization_barrier((swap_pair(low(grad_part)), low(d_dec), d_dec_bias))
    pre_grad = (add(grad_part, arrived) + loss_scale * sparsity * norm_sum[:, :lats]) * factor
    d_enc = dot(low(pre_grad), act, (0, 0))
    d_enc_bias = jnp.sum(pre_grad, axis=0)
    return low(d_enc)[None], d_dec[None], d_enc_bias, d_dec_bias


def solution(mesh):
    placed = (
        P("pair", "lat", None),
        P("pair", "lat", None),
        P("lat"),
        P("pair", "lat", None),
        P("pair", None),
        P("lat"),
        P("lat"),
    )
    return jax.shard_map(
        on_device,
        mesh=mesh,
        in_specs=placed,
        out_specs=(P("pair", "lat", None), P("pair", "lat", None), P("lat"), P("pair", None)),
        check_vma=False,
    )
```

```python
import jax
import jax.numpy as jnp
import numpy as np
from jax import lax
from jax.experimental import pallas as pl
from jax.experimental.pallas import tpu as pltpu
from jax.sharding import PartitionSpec as P

BLK = 128
NZ, NX, NY, NC = 8, 4, 2, 2

epsilon = 1e-06
sparsity = 0.25
loss_scale = 0.0625

EVEN_Z = ((0, 0, 0), (2, 0, 0), (6, 0, 0), (4, 0, 0))
EVEN_XY = ((0, 0, 0), (0, 0, 1), (0, 2, 0), (0, 2, 1))
TURNS = [[(0, 1, 3, 2)[(i - own) % 4] for i in range(4)] for own in range(4)]
TURNS += [[i ^ own for i in range(4)] for own in range(4)]
OCTET_Z = np.array([dz + 2 * k for dz in (0, 0, -1, -1) for k in (0, 1, 3, 2)], np.int32)


def place(z, x, y, c):
    return (((z % NZ) * NX + x % NX) * NY + y % NY) * NC + c % NC


def fetch(value, *offsets, c=0):
    pairs = []
    for iz in range(NZ):
        for ix in range(NX):
            for iy in range(NY):
                for ic in range(NC):
                    z, x, y = offsets[ic % len(offsets)]
                    pairs.append((place(iz + z, ix + x, iy + y, ic + c), place(iz, ix, iy, ic)))
    return lax.ppermute(value, "lat", pairs)


def swap_core(value):
    return fetch(value, (0, 0, 0), c=1)


def pack(pieces):
    rows = [piece.shape[0] for piece in pieces]

    def kernel(*refs):
        at = 0
        for ref, count in zip(refs[:-1], rows):
            refs[-1][at : at + count, :] = ref[...]
            at += count

    return pl.pallas_call(
        kernel,
        out_shape=jax.ShapeDtypeStruct((sum(rows), pieces[0].shape[1]), pieces[0].dtype),
        in_specs=[pl.BlockSpec(memory_space=pltpu.VMEM)] * len(pieces),
        out_specs=pl.BlockSpec(memory_space=pltpu.VMEM),
        compiler_params=pltpu.CompilerParams(vmem_limit_bytes=32 * 1024 * 1024),
    )(*pieces)


def position():
    at = lax.axis_index("lat")
    return at // (NX * NY * NC), at // (NY * NC) % NX, at // NC % NY, at % NC


def by_partner(value):
    near = [value] + [fetch(value, EVEN_Z[k], EVEN_XY[k]) for k in (1, 2, 3)]
    z, x, y, core = position()
    own = jnp.where(core == 0, z // 2, 4 + x // 2 * 2 + y)
    return [lax.select_n(own, *[near[turn[i]] for turn in TURNS]) for i in range(4)]


AROUND = (((0, 1, 0), (0, -1, 0)), ((1, 0, 0), (-1, 0, 0)), ((1, 1, 0), (-1, -1, 0)))


def gather_rows(octet, beside):
    group = pack([octet] + [fetch(octet, EVEN_XY[k], EVEN_Z[k]) for k in (1, 2, 3)])
    groups = [group] + [fetch(group, *to) for to in AROUND]
    others = [swap_core(each) for each in groups]
    half = beside([groups[0], groups[3], others[0], others[3]])
    others[1], half = lax.optimization_barrier((others[1], half))
    return groups + others, half


def low(value):
    return value.astype(jnp.bfloat16)


def add(value, arrived):
    return value + arrived.astype(jnp.float32)


def scatter_rows(latent, dec):
    rows = latent.shape[0] // 2
    theirs = low(dot(latent[rows:], dec, (1, 0)))
    mine = dot(latent[:rows], dec, (1, 0))
    sent = low(add(mine[96:], swap_core(theirs[96:])))
    next_to, _ = lax.optimization_barrier((swap_core(theirs[32:96]), sent))
    last, next_to = lax.optimization_barrier((theirs[:32], next_to))
    rest = add(mine[32:96], next_to)
    group = add(mine[:32], swap_core(last))
    group = add(group, fetch(sent, *AROUND[2][::-1]))
    group = add(group, fetch(low(rest[32:]), *AROUND[1][::-1]))
    group = add(group, fetch(low(rest[:32]), *AROUND[0][::-1]))
    octet = group[0:8]
    for k, back in ((3, 3), (2, 1), (1, 2)):
        octet = add(octet, fetch(low(group[8 * k : 8 * k + 8]), EVEN_XY[k], EVEN_Z[back]))
    parts = [part.astype(jnp.float32) for part in by_partner(low(octet))]
    return parts[0] + parts[1] + parts[2] + parts[3]


def swap_pair(value):
    return lax.ppermute(value, "pair", [(0, 1), (1, 0)])


def dot(left, right, over):
    return lax.dot_general(left, right, ((over[:1], over[1:]), ((), ())), preferred_element_type=jnp.float32)


def total_rows(groups):
    rows = pack(groups)
    return dot(jnp.ones((8, rows.shape[0]), rows.dtype), rows, (1, 0))[0:1]


def on_device(activations, enc_weight, enc_bias, dec_weight, dec_bias, block_list, block_count):
    enc, dec = enc_weight[0], dec_weight[0]
    own = activations[0]
    tokens = 2 * BLK
    own_octet = jnp.concatenate(by_partner(own), axis=0)
    norm_own = jnp.sqrt(jnp.sum(jnp.square(dec.astype(jnp.float32)), axis=1) + epsilon)
    act_groups, norm_own = gather_rows(own_octet, lambda _: norm_own)

    slots = jnp.arange(block_list.shape[0], dtype=jnp.int32) < block_count[0]
    z, _, _, core = position()
    by_octet = jnp.repeat((z + OCTET_Z) % NZ, 8)
    kinds = [jnp.tile(jnp.arange(NZ, dtype=jnp.int32), tokens // 2 // NZ), by_octet]
    z_row = jnp.concatenate([jnp.where(core == own, kinds[0], kinds[1]) for own in (0, 1)])
    block = z_row // (NZ // 2)
    live = jnp.any((block[:, None] == block_list[None, :]) & slots[None, :], axis=1)
    live = live.astype(jnp.float32)[:, None]

    act_halves = [pack(act_groups[:4]), pack(act_groups[4:])]
    pre_part = [dot(half, enc, (1, 1)) for half in act_halves]
    packed = jnp.concatenate(pre_part + [jnp.broadcast_to(norm_own[None, :], (8, norm_own.shape[0]))], axis=0)
    arrived, act = lax.optimization_barrier((swap_pair(low(packed)), pack(act_halves)))
    packed = add(packed, arrived)
    norm_sum = packed[tokens : tokens + 1]
    pre_act = packed[:tokens] + enc_bias[None, :]
    latent_act = jax.nn.softplus(pre_act) * live
    latent_low = low(latent_act)

    rebuilt = scatter_rows(latent_low, dec) + dec_bias
    slope = loss_scale * sparsity * jnp.sum(latent_act, axis=0) / norm_own
    factor, slope = lax.optimization_barrier((jax.nn.sigmoid(pre_act) * live, slope))
    err_groups, bias_part = gather_rows(low(loss_scale * (rebuilt - own_octet.astype(jnp.float32))), total_rows)

    err_halves = [pack(err_groups[:4]), pack(err_groups[4:])]
    grad_part = jnp.concatenate([dot(half, dec, (1, 1)) for half in err_halves], axis=0)
    err = pack(err_halves)
    d_dec = dot(latent_low, err, (0, 0)) + slope[:, None] * dec.astype(jnp.float32)
    d_dec_bias = bias_part + total_rows([err_groups[k] for k in (1, 2, 5, 6)])
    arrived, d_dec, d_dec_bias = lax.optimization_barrier((swap_pair(low(grad_part)), low(d_dec), d_dec_bias))
    pre_grad = (add(grad_part, arrived) + loss_scale * sparsity * norm_sum) * factor
    pre_low = low(pre_grad)
    d_enc = dot(pre_low, act, (0, 0))
    d_enc_bias = jnp.sum(pre_grad, axis=0)
    return low(d_enc)[None], d_dec[None], d_enc_bias, d_dec_bias


def solution(mesh):
    placed = (
        P("pair", "lat", None),
        P("pair", "lat", None),
        P("lat"),
        P("pair", "lat", None),
        P("pair", None),
        P("lat"),
        P("lat"),
    )
    return jax.shard_map(
        on_device,
        mesh=mesh,
        in_specs=placed,
        out_specs=(P("pair", "lat", None), P("pair", "lat", None), P("lat"), P("pair", None)),
        check_vma=False,
    )
```

```python
import jax
import jax.numpy as jnp
import numpy as np
from jax import lax
from jax.experimental import pallas as pl
from jax.experimental.pallas import tpu as pltpu
from jax.sharding import PartitionSpec as P

BLK = 128
NZ, NX, NY, NC = 8, 4, 2, 2

epsilon = 1e-06
sparsity = 0.25
loss_scale = 0.0625

EVEN_Z = ((0, 0, 0), (2, 0, 0), (6, 0, 0), (4, 0, 0))
EVEN_XY = ((0, 0, 0), (0, 0, 1), (0, 2, 0), (0, 2, 1))
TURNS = [[(0, 1, 3, 2)[(i - own) % 4] for i in range(4)] for own in range(4)]
TURNS += [[i ^ own for i in range(4)] for own in range(4)]
OCTET_Z = np.array([dz + 2 * k for dz in (0, 0, -1, 1) for k in (0, 1, 3, 2)], np.int32)


def place(z, x, y, c):
    return (((z % NZ) * NX + x % NX) * NY + y % NY) * NC + c % NC


def fetch(value, *offsets, c=0):
    pairs = []
    for iz in range(NZ):
        for ix in range(NX):
            for iy in range(NY):
                for ic in range(NC):
                    z, x, y = offsets[ic % len(offsets)]
                    pairs.append((place(iz + z, ix + x, iy + y, ic + c), place(iz, ix, iy, ic)))
    return lax.ppermute(value, "lat", pairs)


def swap_core(value):
    return fetch(value, (0, 0, 0), c=1)


def pack(pieces):
    rows = [piece.shape[0] for piece in pieces]

    def kernel(*refs):
        at = 0
        for ref, count in zip(refs[:-1], rows):
            refs[-1][at : at + count, :] = ref[...]
            at += count

    return pl.pallas_call(
        kernel,
        out_shape=jax.ShapeDtypeStruct((sum(rows), pieces[0].shape[1]), pieces[0].dtype),
        in_specs=[pl.BlockSpec(memory_space=pltpu.VMEM)] * len(pieces),
        out_specs=pl.BlockSpec(memory_space=pltpu.VMEM),
        compiler_params=pltpu.CompilerParams(vmem_limit_bytes=32 * 1024 * 1024),
    )(*pieces)


def position():
    at = lax.axis_index("lat")
    return at // (NX * NY * NC), at // (NY * NC) % NX, at // NC % NY, at % NC


def by_partner(value):
    near = [value] + [fetch(value, EVEN_Z[k], EVEN_XY[k]) for k in (1, 2, 3)]
    z, x, y, core = position()
    own = jnp.where(core == 0, z // 2, 4 + x // 2 * 2 + y)
    return [lax.select_n(own, *[near[turn[i]] for turn in TURNS]) for i in range(4)]


AROUND = (((0, 1, 0), (0, -1, 0)), ((1, 0, 0), (-1, 0, 0)), ((-1, 1, 0), (1, -1, 0)))


def gather_rows(octet):
    group = pack([octet] + [fetch(octet, EVEN_XY[k], EVEN_Z[k]) for k in (1, 2, 3)])
    groups = [group] + [fetch(group, *to) for to in AROUND]
    return groups + [swap_core(each) for each in groups]


def low(value):
    return value.astype(jnp.bfloat16)


def add(value, arrived):
    return value + arrived.astype(jnp.float32)


def scatter_rows(latent, dec):
    rows = latent.shape[0] // 2
    theirs = low(dot(latent[rows:], dec, (1, 0)))
    mine = dot(latent[:rows], dec, (1, 0))
    sent = low(add(mine[96:], swap_core(theirs[96:])))
    theirs, sent = lax.optimization_barrier((theirs[:96], sent))
    rest = add(mine[:96], swap_core(theirs))
    group = add(rest[:32], fetch(sent, *AROUND[2][::-1]))
    group = add(group, fetch(low(rest[64:]), *AROUND[1][::-1]))
    group = add(group, fetch(low(rest[32:64]), *AROUND[0][::-1]))
    octet = group[0:8]
    for k, back in ((3, 3), (2, 1), (1, 2)):
        octet = add(octet, fetch(low(group[8 * k : 8 * k + 8]), EVEN_XY[k], EVEN_Z[back]))
    parts = [part.astype(jnp.float32) for part in by_partner(low(octet))]
    return parts[0] + parts[1] + parts[2] + parts[3]


def swap_pair(value):
    return lax.ppermute(value, "pair", [(0, 1), (1, 0)])


def dot(left, right, over):
    return lax.dot_general(left, right, ((over[:1], over[1:]), ((), ())), preferred_element_type=jnp.float32)


def on_device(activations, enc_weight, enc_bias, dec_weight, dec_bias, block_list, block_count):
    enc, dec = enc_weight[0], dec_weight[0]
    own = activations[0]
    tokens = 2 * BLK
    norm_own = jnp.sqrt(jnp.sum(jnp.square(dec.astype(jnp.float32)), axis=1) + epsilon)
    own_octet = jnp.concatenate(by_partner(own), axis=0)
    act_groups = gather_rows(own_octet)

    slots = jnp.arange(block_list.shape[0], dtype=jnp.int32) < block_count[0]
    z, _, _, core = position()
    by_octet = jnp.repeat((z + OCTET_Z) % NZ, 8)
    kinds = [jnp.tile(jnp.arange(NZ, dtype=jnp.int32), tokens // 2 // NZ), by_octet]
    z_row = jnp.concatenate([jnp.where(core == own, kinds[0], kinds[1]) for own in (0, 1)])
    block = z_row // (NZ // 2)
    live = jnp.any((block[:, None] == block_list[None, :]) & slots[None, :], axis=1)
    live = live.astype(jnp.float32)[:, None]

    act_halves = [pack(act_groups[:4]), pack(act_groups[4:])]
    pre_part = [dot(half, enc, (1, 1)) for half in act_halves]
    packed = jnp.concatenate(pre_part + [jnp.broadcast_to(norm_own[None, :], (8, norm_own.shape[0]))], axis=0)
    arrived, act = lax.optimization_barrier((swap_pair(low(packed)), pack(act_halves)))
    packed = add(packed, arrived)
    norm_sum = packed[tokens : tokens + 1]
    pre_act = packed[:tokens] + enc_bias[None, :]
    latent_act = jax.nn.softplus(pre_act) * live
    latent_low = low(latent_act)

    rebuilt = scatter_rows(latent_low, dec) + dec_bias
    err_groups = gather_rows(low(loss_scale * (rebuilt - own_octet.astype(jnp.float32))))

    err_halves = [pack(err_groups[:4]), pack(err_groups[4:])]
    grad_part = jnp.concatenate([dot(half, dec, (1, 1)) for half in err_halves], axis=0)
    err = pack(err_halves)
    act_total = jnp.sum(latent_act, axis=0)
    d_dec = dot(latent_low, err, (0, 0))
    d_dec = d_dec + (loss_scale * sparsity * act_total / norm_own)[:, None] * dec.astype(jnp.float32)
    d_dec_bias = dot(jnp.ones((8, tokens), jnp.bfloat16), err, (1, 0))[0:1]
    arrived, d_dec, d_dec_bias = lax.optimization_barrier((swap_pair(low(grad_part)), low(d_dec), d_dec_bias))
    grad_sum = add(grad_part, arrived)
    grad_latent = (grad_sum + loss_scale * sparsity * norm_sum) * live
    pre_grad = grad_latent * jax.nn.sigmoid(pre_act)
    pre_low = low(pre_grad)

    d_enc = dot(pre_low, act, (0, 0))
    d_enc_bias = jnp.sum(pre_grad, axis=0)
    return low(d_enc)[None], d_dec[None], d_enc_bias, d_dec_bias


def solution(mesh):
    placed = (
        P("pair", "lat", None),
        P("pair", "lat", None),
        P("lat"),
        P("pair", "lat", None),
        P("pair", None),
        P("lat"),
        P("lat"),
    )
    return jax.shard_map(
        on_device,
        mesh=mesh,
        in_specs=placed,
        out_specs=(P("pair", "lat", None), P("pair", "lat", None), P("lat"), P("pair", None)),
        check_vma=False,
    )
```
